32 devices in a mesh: band: 8 (over z, x), sub: 4 (over y, core).
Axes of the slice: x: 2, y: 2, z: 4, core: 2. Of those that a mesh axis runs over, the one named last changes fastest.
Arguments:
- atmos_flux: bfloat16 [32, 64, 512], P(None, 'band', 'sub'), may hold values from -6 to 6
- weight_tiles: bfloat16 [8, 4, 32, 384, 128], P('band', 'sub'), may hold values from -0.3125 to 0.3125
- source_row: int32 [8, 4, 32], P('band', 'sub'), may hold values from 0 to 7
- target_code: int32 [8, 4, 32], P('band', 'sub'), may hold values from 0 to 63
- live_count: int32 [8, 4], P('band', 'sub'), may hold values from 8 to 32, as said below
Outputs:
- ocean_flux: float32 [32, 32768], P(None, ('band', 'sub'))
The draws below stay inside these ranges and needn't reach their ends.
Inputs may be any that keep to these rules, and one draw needn't show every extreme that they name: `live_count`: each device has between 8 and 32 live entries; some device has exactly 32.
All inputs are finite; a program needn't handle non-finite values.
Results may differ from the reference program's by a relative error of at most 0.0036.
Values may be sent and summed in bfloat16 or wider, within the bound.
A program may use at most 64 MiB of HBM per device.

```python
import jax
import jax.numpy as jnp
from jax import lax

FIELDS = 8
TIMES = 4
LON_DEV = 128
LAT_DEV = 8
OB_DEV = 8
OV_CAP = 32
LAT = 64
LON = 512
N_BAND = 8
N_SUB = 4


def draw_live_count(key, part):
    key = jax.random.fold_in(key, 7)
    first, second, third, fourth = jax.random.split(key, 4)
    shape = (N_BAND, N_SUB)
    inland = jax.random.randint(first, shape, OV_CAP // 4, OV_CAP // 2 + 1)
    coastal = jax.random.randint(second, shape, 3 * OV_CAP // 4, OV_CAP + 1)
    is_coast = jax.random.randint(third, shape, 0, 8) == 0
    counts = jnp.where(is_coast, coastal, inland).reshape(-1)
    chosen = jax.random.randint(fourth, (), 0, N_BAND * N_SUB)
    counts = jnp.where(jnp.arange(N_BAND * N_SUB) == chosen, OV_CAP, counts)
    return counts.reshape(shape).astype(jnp.int32)


def set_ends(values, rng, low, high):
    spot = [jax.random.randint(jax.random.fold_in(rng, axis), (), 0, length) for axis, length in enumerate(values.shape)]
    longest = values.shape.index(max(values.shape))
    next_to = spot[:longest] + [(spot[longest] + 1) % values.shape[longest]] + spot[longest + 1:]
    return values.at[tuple(spot)].set(low).at[tuple(next_to)].set(high)


def block_levels(key, extent, cuts, smallest, top_value):
    level = 1.0
    for position, parts in cuts:
        heights = jax.random.uniform(jax.random.fold_in(jax.random.fold_in(key, 6), position), (parts,), jnp.float32, smallest / len(cuts), top_value / len(cuts))
        level = level * jnp.repeat(jnp.exp(heights), extent[position] // parts).reshape((-1,) + (1,) * (len(extent) - 1 - position))
    return level


def centred(own_key, dims, scale, most, shards=(), kind=jnp.bfloat16):
    result = jax.random.normal(own_key, dims, jnp.float32) * scale
    if len(shards) > 0:
        result = block_levels(own_key, dims, shards, -0.22, 0.18) * result
    return jnp.clip(result, min=-most, max=most).astype(kind)


def setup_inputs(seed: int = 0) -> dict:
    keys = jax.random.split(jax.random.key(seed), 6)
    atmos_flux = centred(keys[0], (FIELDS * TIMES, LAT, LON), 1.0, 6.0, ((1, 8), (2, 4)))
    weight_tiles = centred(keys[1], (N_BAND, N_SUB, OV_CAP, 3 * LON_DEV, LON_DEV), (3 * LON_DEV) ** -0.5, 0.3125, ((0, 8), (1, 4)))
    source_row = set_ends(jax.random.randint(keys[2], (N_BAND, N_SUB, OV_CAP), 0, LAT_DEV), jax.random.fold_in(keys[2], 1), 0, LAT_DEV - 1).astype(jnp.int32)
    target_code = set_ends(jax.random.randint(keys[3], (N_BAND, N_SUB, OV_CAP), 0, 2 * N_SUB * OB_DEV), jax.random.fold_in(keys[3], 1), 0, (2 * N_SUB * OB_DEV) - 1).astype(jnp.int32)
    live_count = draw_live_count(jax.random.fold_in(keys[5], 71), 0)
    return dict(atmos_flux=atmos_flux, weight_tiles=weight_tiles, source_row=source_row, target_code=target_code, live_count=live_count)


def reference(atmos_flux, weight_tiles, source_row, target_code, live_count):
    fields = FIELDS * TIMES
    widened = jnp.pad(atmos_flux.astype(jnp.float32), ((0, 0), (1, 1), (1, 1)))
    grad_x = (0.5 * (widened[:, 1:-1, 2:] - widened[:, 1:-1, :-2])).astype(jnp.bfloat16)
    grad_y = (0.5 * (widened[:, 2:, 1:-1] - widened[:, :-2, 1:-1])).astype(jnp.bfloat16)

    def blocks(whole):
        shaped = whole.reshape(fields, N_BAND, LAT_DEV, N_SUB, LON_DEV)
        return shaped.transpose(1, 3, 2, 0, 4).reshape(N_BAND * N_SUB, LAT_DEV, fields, LON_DEV)

    operand = jnp.concatenate([blocks(atmos_flux), blocks(grad_x), blocks(grad_y)], axis=-1)
    targets = 2 * N_SUB * OB_DEV

    def one_device(items):
        rows_op, tiles_dev, rows_idx, codes, count_dev = items
        picked = rows_op[rows_idx]
        product = jnp.einsum("ekc,ecl->ekl", picked.astype(jnp.float32), tiles_dev.astype(jnp.float32), precision=lax.Precision.HIGHEST)
        live = (jnp.arange(OV_CAP, dtype=jnp.int32) < count_dev).astype(jnp.float32)
        selector = (codes[None, :] == jnp.arange(targets, dtype=jnp.int32)[:, None]).astype(jnp.float32) * live[None, :]
        summed = jnp.einsum("te,ekl->tkl", selector, product, precision=lax.Precision.HIGHEST)
        return summed.astype(jnp.bfloat16)

    partial_all = lax.map(one_device, (operand,
                                       weight_tiles.reshape(N_BAND * N_SUB, OV_CAP, 3 * LON_DEV, LON_DEV),
                                       source_row.reshape(N_BAND * N_SUB, OV_CAP),
                                       target_code.reshape(N_BAND * N_SUB, OV_CAP),
                                       live_count.reshape(N_BAND * N_SUB)))
    partial_all = partial_all.astype(jnp.float32).reshape(N_BAND, N_SUB, N_SUB, 2, OB_DEV, fields, LON_DEV)
    own_band = jnp.sum(partial_all[:, :, :, 0], axis=1)
    next_band = jnp.roll(jnp.sum(partial_all[:, :, :, 1], axis=1), 1, axis=0)
    total = own_band + next_band
    return total.transpose(3, 0, 1, 2, 4).reshape(fields, N_BAND * N_SUB * OB_DEV * LON_DEV)
```

```python
import functools

import jax
import jax.numpy as jnp
from jax import lax
from jax.experimental import pallas as pl
from jax.experimental.pallas import tpu as pltpu
from jax.sharding import PartitionSpec as P

OB_DEV = 8
MESH = pl.DeviceIdType.MESH


def kernel(
    sizes, idx_ref, flux_ref, weight_ref, out_ref,
    xin, x32, op, wv, prefix, halo_out, halo_in, a_out, a_in, b_out, b_in,
    in_sem, halo_send, halo_recv, a_send, a_recv, b_send, b_recv,
):
    fields, rows, width, cap, bands, subs = sizes
    ny = subs // 2
    b = lax.axis_index("band")
    s = lax.axis_index("sub")
    y, core = s // 2, s % 2
    up, down = (b + 1) % bands, (b + bands - 1) % bands

    copy_flux = pltpu.make_async_copy(flux_ref, xin, in_sem.at[0])
    copy_flux.start()
    copy_w0 = pltpu.make_async_copy(weight_ref.at[:, :width], wv.at[:, :width], in_sem.at[1])
    copy_w0.start()
    half = cap // 2
    copy_w = []
    for part in range(2):
        where = (pl.ds(part * half, half), pl.ds(width, 2 * width))
        copy_w.append(pltpu.make_async_copy(weight_ref.at[where], wv.at[where], in_sem.at[2 + part]))
        copy_w[-1].start()

    barrier = pltpu.get_barrier_semaphore()
    for other in range(1, subs):
        pl.semaphore_signal(barrier, inc=1, device_id=(b, (s + other) % subs), device_id_type=MESH)
    for other in range(ny):
        pl.semaphore_signal(barrier, inc=1, device_id=(up, other * 2 + core), device_id_type=MESH)
        pl.semaphore_signal(barrier, inc=1, device_id=(down, other * 2 + core), device_id_type=MESH)

    copy_flux.wait()
    x32[...] = xin[...].astype(jnp.float32)
    lane = lax.broadcasted_iota(jnp.int32, (fields, width), 1)

    def row(i):
        return x32[pl.ds(i, fields, stride=rows), :]

    first = jnp.zeros((fields, width), jnp.float32)
    last = jnp.zeros((fields, width), jnp.float32)
    for i in range(rows):
        x = row(i)
        op[i, :, :width] = x.astype(jnp.bfloat16)
        first = jnp.where(lane == i, x[:, :1], first)
        last = jnp.where(lane == i, x[:, width - 1:], last)
    halo_out[0] = row(rows - 1).astype(jnp.bfloat16)
    halo_out[1] = row(0).astype(jnp.bfloat16)
    halo_out[2] = last.astype(jnp.bfloat16)
    halo_out[3] = first.astype(jnp.bfloat16)
    prefix[cap] = jnp.zeros((fields, width), jnp.float32)

    pl.semaphore_wait(barrier, subs - 1 + 2 * ny)

    partners = ((up, s), (down, s), (b, (s + 1) % subs), (b, (s + subs - 1) % subs))
    sends = (b < bands - 1, b > 0, s < subs - 1, s > 0)
    receives = (b > 0, b < bands - 1, s > 0, s < subs - 1)
    halos = [
        pltpu.make_async_remote_copy(
            src_ref=halo_out.at[k], dst_ref=halo_in.at[k], send_sem=halo_send.at[k], recv_sem=halo_recv.at[k],
            device_id=partners[k], device_id_type=MESH)
        for k in range(4)
    ]
    for k in range(4):
        @pl.when(sends[k])
        def _(k=k):
            halos[k].start()

    copy_w0.wait()

    def flux_part(e, carry):
        picked = op[idx_ref[e], :, :width]
        prefix[e] = jnp.dot(picked, wv[e, :width], preferred_element_type=jnp.float32)
        return carry

    lax.fori_loop(0, cap, flux_part, 0, unroll=True)

    for k in range(4):
        @pl.when(receives[k])
        def _(k=k):
            halos[k].wait_recv()

        @pl.when(jnp.logical_not(receives[k]))
        def _(k=k):
            halo_in[k] = jnp.zeros((fields, width), jnp.bfloat16)

    below, above, left, right = (halo_in[k].astype(jnp.float32) for k in range(4))
    for i in range(rows):
        x = row(i)
        before = row(i - 1) if i > 0 else below
        after = row(i + 1) if i < rows - 1 else above
        west = jnp.where(lane == 0, left[:, i:i + 1], pltpu.roll(x, 1, 1))
        east = jnp.where(lane == width - 1, right[:, i:i + 1], pltpu.roll(x, width - 1, 1))
        op[i, :, width:2 * width] = (0.5 * (east - west)).astype(jnp.bfloat16)
        op[i, :, 2 * width:] = (0.5 * (after - before)).astype(jnp.bfloat16)

    def gradient_part(e, carry):
        picked = op[idx_ref[e], :, width:]
        product = jnp.dot(picked, wv[e, width:], preferred_element_type=jnp.float32)
        prefix[e] = prefix[e] + product + prefix[idx_ref[cap + e]]
        return carry

    for part in range(2):
        copy_w[part].wait()
        lax.fori_loop(part * half, (part + 1) * half, gradient_part, 0, unroll=True)

    def partial(sub, step, q):
        return prefix[idx_ref[2 * cap + (sub * 2 + step) * OB_DEV + q]]

    pieces = [(j, 1) for j in range(1, ny)] + [(0, 1)] + [(j, 0) for j in range(1, ny)] + [(0, 0)]
    swaps, moves = [], []
    for p, (j, step) in enumerate(pieces):
        target = (y + j) % ny * 2 + 1 - core
        for q in range(OB_DEV):
            a_out[p, q] = partial(target, step, q).astype(jnp.bfloat16)
        swaps.append(pltpu.make_async_remote_copy(
            src_ref=a_out.at[p], dst_ref=a_in.at[p], send_sem=a_send.at[p], recv_sem=a_recv.at[p],
            device_id=(b, y * 2 + 1 - core), device_id_type=MESH))
        swaps[-1].start()
    for p, (j, step) in enumerate(pieces):
        target = (y + j) % ny * 2 + core
        swaps[p].wait_recv()
        if (j, step) == (0, 0):
            for q in range(OB_DEV):
                out_ref[:, q * width:(q + 1) * width] = partial(target, step, q) + a_in[p, q].astype(jnp.float32)
            continue
        for q in range(OB_DEV):
            b_out[p, q] = (partial(target, step, q) + a_in[p, q].astype(jnp.float32)).astype(jnp.bfloat16)
        moves.append(pltpu.make_async_remote_copy(
            src_ref=b_out.at[p], dst_ref=b_in.at[p], send_sem=b_send.at[p], recv_sem=b_recv.at[p],
            device_id=(up if step else b, target), device_id_type=MESH))
        moves[-1].start()
    for move in moves:
        move.wait_recv()
    for q in range(OB_DEV):
        total = out_ref[:, q * width:(q + 1) * width]
        for p in range(len(moves)):
            total = total + b_in[p, q].astype(jnp.float32)
        out_ref[:, q * width:(q + 1) * width] = total

    for k in range(4):
        @pl.when(sends[k])
        def _(k=k):
            halos[k].wait_send()
    for copy in swaps + moves:
        copy.wait_send()


def shards(atmos_flux, weight_tiles, source_row, target_code, live_count):
    fields, rows, width = atmos_flux.shape
    cap = weight_tiles.shape[2]
    bands, subs = lax.axis_size("band"), lax.axis_size("sub")
    targets = 2 * subs * OB_DEV
    pieces = subs

    code = target_code[0, 0]
    entry = jnp.arange(cap, dtype=jnp.int32)
    wanted = jnp.concatenate([code, jnp.arange(targets, dtype=jnp.int32)])
    limit = jnp.concatenate([entry, jnp.full((targets,), live_count[0, 0], jnp.int32)])
    match = (wanted[:, None] == code[None, :]) & (entry[None, :] < limit[:, None])
    found = jnp.max(jnp.where(match, entry[None, :], -1), axis=1)
    found = jnp.where(found < 0, cap, found)
    table = jnp.concatenate([source_row[0, 0], found])

    block = (OB_DEV, fields, width)
    return pl.pallas_call(
        functools.partial(kernel, (fields, rows, width, cap, bands, subs)),
        out_shape=jax.ShapeDtypeStruct((fields, OB_DEV * width), jnp.float32),
        in_specs=[
            pl.BlockSpec(memory_space=pltpu.SMEM),
            pl.BlockSpec(memory_space=pltpu.HBM),
            pl.BlockSpec(memory_space=pltpu.HBM),
        ],
        out_specs=pl.BlockSpec(memory_space=pltpu.VMEM),
        scratch_shapes=[
            pltpu.VMEM((fields * rows, width), jnp.bfloat16),
            pltpu.VMEM((fields * rows, width), jnp.float32),
            pltpu.VMEM((rows, fields, 3 * width), jnp.bfloat16),
            pltpu.VMEM((cap, 3 * width, width), jnp.bfloat16),
            pltpu.VMEM((cap + 1, fields, width), jnp.float32),
            pltpu.VMEM((4, fields, width), jnp.bfloat16),
            pltpu.VMEM((4, fields, width), jnp.bfloat16),
            pltpu.VMEM((pieces,) + block, jnp.bfloat16),
            pltpu.VMEM((pieces,) + block, jnp.bfloat16),
            pltpu.VMEM((pieces - 1,) + block, jnp.bfloat16),
            pltpu.VMEM((pieces - 1,) + block, jnp.bfloat16),
            pltpu.SemaphoreType.DMA((4,)),
            pltpu.SemaphoreType.DMA((4,)),
            pltpu.SemaphoreType.DMA((4,)),
            pltpu.SemaphoreType.DMA((pieces,)),
            pltpu.SemaphoreType.DMA((pieces,)),
            pltpu.SemaphoreType.DMA((pieces - 1,)),
            pltpu.SemaphoreType.DMA((pieces - 1,)),
        ],
        compiler_params=pltpu.CompilerParams(
            collective_id=0, has_side_effects=True, vmem_limit_bytes=24 * 1024 * 1024
        ),
    )(table, atmos_flux.reshape(fields * rows, width), weight_tiles[0, 0])


def solution(mesh):
    return jax.shard_map(
        shards,
        mesh=mesh,
        in_specs=(
            P(None, "band", "sub"),
            P("band", "sub", None, None, None),
            P("band", "sub", None),
            P("band", "sub", None),
            P("band", "sub"),
        ),
        out_specs=P(None, ("band", "sub")),
        check_vma=False,
    )
```

```python
import functools

import jax
import jax.numpy as jnp
from jax import lax
from jax.experimental import pallas as pl
from jax.experimental.pallas import tpu as pltpu
from jax.sharding import PartitionSpec as P

OB_DEV = 8
MESH = pl.DeviceIdType.MESH


def kernel(
    sizes, row_ref, code_ref, live_ref, flux_ref, weight_ref, out_ref,
    table, found, xin, x32, op, wv, prefix, halo_out, halo_in, a_out, a_in, b_out, b_in,
    in_sem, halo_send, halo_recv, a_send, a_recv, b_send, b_recv,
):
    fields, rows, width, cap, bands, subs = sizes
    ny = subs // 2
    b = lax.axis_index("band")
    s = lax.axis_index("sub")
    y, core = s // 2, s % 2
    up, down = (b + 1) % bands, (b + bands - 1) % bands

    copy_flux = pltpu.make_async_copy(flux_ref, xin, in_sem.at[0])
    copy_flux.start()
    copy_w0 = pltpu.make_async_copy(weight_ref.at[:, :width], wv.at[:, :width], in_sem.at[1])
    copy_w0.start()
    half = cap // 2
    copy_w = []
    for part in range(2):
        where = (pl.ds(part * half, half), pl.ds(width, 2 * width))
        copy_w.append(pltpu.make_async_copy(weight_ref.at[where], wv.at[where], in_sem.at[2 + part]))
        copy_w[-1].start()

    barrier = pltpu.get_barrier_semaphore()
    for other in range(1, subs):
        pl.semaphore_signal(barrier, inc=1, device_id=(b, (s + other) % subs), device_id_type=MESH)
    for other in range(ny):
        pl.semaphore_signal(barrier, inc=1, device_id=(up, other * 2 + core), device_id_type=MESH)
        pl.semaphore_signal(barrier, inc=1, device_id=(down, other * 2 + core), device_id_type=MESH)

    part_row = lax.broadcasted_iota(jnp.int32, table.shape, 0)
    part_lane = lax.broadcasted_iota(jnp.int32, table.shape, 1)
    wanted = (part_row - 1) * table.shape[1] + part_lane
    for e in range(cap):
        wanted = jnp.where((part_row == 0) & (part_lane == e), code_ref[e], wanted)
    limit = jnp.where(part_row == 0, part_lane, live_ref[0, 0])
    entry = jnp.full(table.shape, cap, jnp.int32)
    for e in range(cap):
        entry = jnp.where((wanted == code_ref[e]) & (limit > e), e, entry)
    table[...] = entry
    copy_found = pltpu.make_async_copy(table, found, in_sem.at[4])
    copy_found.start()

    copy_flux.wait()
    x32[...] = xin[...].astype(jnp.float32)
    lane = lax.broadcasted_iota(jnp.int32, (fields, width), 1)

    def row(i):
        return x32[pl.ds(i, fields, stride=rows), :]

    first = jnp.zeros((fields, width), jnp.float32)
    last = jnp.zeros((fields, width), jnp.float32)
    for i in range(rows):
        x = row(i)
        op[i, :, :width] = x.astype(jnp.bfloat16)
        first = jnp.where(lane == i, x[:, :1], first)
        last = jnp.where(lane == i, x[:, width - 1:], last)
    halo_out[0] = row(rows - 1).astype(jnp.bfloat16)
    halo_out[1] = row(0).astype(jnp.bfloat16)
    halo_out[2] = last.astype(jnp.bfloat16)
    halo_out[3] = first.astype(jnp.bfloat16)
    prefix[cap] = jnp.zeros((fields, width), jnp.float32)

    pl.semaphore_wait(barrier, subs - 1 + 2 * ny)

    partners = ((up, s), (down, s), (b, (s + 1) % subs), (b, (s + subs - 1) % subs))
    sends = (b < bands - 1, b > 0, s < subs - 1, s > 0)
    receives = (b > 0, b < bands - 1, s > 0, s < subs - 1)
    halos = [
        pltpu.make_async_remote_copy(
            src_ref=halo_out.at[k], dst_ref=halo_in.at[k], send_sem=halo_send.at[k], recv_sem=halo_recv.at[k],
            device_id=partners[k], device_id_type=MESH)
        for k in range(4)
    ]
    for k in range(4):
        @pl.when(sends[k])
        def _(k=k):
            halos[k].start()

    copy_w0.wait()

    def flux_part(e, carry):
        picked = op[row_ref[e], :, :width]
        prefix[e] = jnp.dot(picked, wv[e, :width], preferred_element_type=jnp.float32)
        return carry

    lax.fori_loop(0, cap, flux_part, 0, unroll=True)

    for k in range(4):
        @pl.when(receives[k])
        def _(k=k):
            halos[k].wait_recv()

        @pl.when(jnp.logical_not(receives[k]))
        def _(k=k):
            halo_in[k] = jnp.zeros((fields, width), jnp.bfloat16)

    below, above, left, right = (halo_in[k].astype(jnp.float32) for k in range(4))
    for i in range(rows):
        x = row(i)
        before = row(i - 1) if i > 0 else below
        after = row(i + 1) if i < rows - 1 else above
        west = jnp.where(lane == 0, left[:, i:i + 1], pltpu.roll(x, 1, 1))
        east = jnp.where(lane == width - 1, right[:, i:i + 1], pltpu.roll(x, width - 1, 1))
        op[i, :, width:2 * width] = (0.5 * (east - west)).astype(jnp.bfloat16)
        op[i, :, 2 * width:] = (0.5 * (after - before)).astype(jnp.bfloat16)

    def gradient_part(e, carry):
        picked = op[row_ref[e], :, width:]
        product = jnp.dot(picked, wv[e, width:], preferred_element_type=jnp.float32)
        prefix[e] = prefix[e] + product + prefix[found[0, e]]
        return carry

    copy_found.wait()
    for part in range(2):
        copy_w[part].wait()
        lax.fori_loop(part * half, (part + 1) * half, gradient_part, 0, unroll=True)

    def partial(sub, step, q):
        t = (sub * 2 + step) * OB_DEV + q
        return prefix[found[1 + t // found.shape[1], t % found.shape[1]]]

    pieces = [(j, 1) for j in range(1, ny)] + [(0, 1)] + [(j, 0) for j in range(1, ny)] + [(0, 0)]
    swaps, moves = [], []
    for p, (j, step) in enumerate(pieces):
        target = (y + j) % ny * 2 + 1 - core
        for q in range(OB_DEV):
            a_out[p, q] = partial(target, step, q).astype(jnp.bfloat16)
        swaps.append(pltpu.make_async_remote_copy(
            src_ref=a_out.at[p], dst_ref=a_in.at[p], send_sem=a_send.at[p], recv_sem=a_recv.at[p],
            device_id=(b, y * 2 + 1 - core), device_id_type=MESH))
        swaps[-1].start()
    for p, (j, step) in enumerate(pieces):
        target = (y + j) % ny * 2 + core
        swaps[p].wait_recv()
        if (j, step) == (0, 0):
            for q in range(OB_DEV):
                out_ref[:, q * width:(q + 1) * width] = partial(target, step, q) + a_in[p, q].astype(jnp.float32)
            continue
        for q in range(OB_DEV):
            b_out[p, q] = (partial(target, step, q) + a_in[p, q].astype(jnp.float32)).astype(jnp.bfloat16)
        moves.append(pltpu.make_async_remote_copy(
            src_ref=b_out.at[p], dst_ref=b_in.at[p], send_sem=b_send.at[p], recv_sem=b_recv.at[p],
            device_id=(up if step else b, target), device_id_type=MESH))
        moves[-1].start()
    for move in moves:
        move.wait_recv()
    for q in range(OB_DEV):
        total = out_ref[:, q * width:(q + 1) * width]
        for p in range(len(moves)):
            total = total + b_in[p, q].astype(jnp.float32)
        out_ref[:, q * width:(q + 1) * width] = total

    for k in range(4):
        @pl.when(sends[k])
        def _(k=k):
            halos[k].wait_send()
    for copy in swaps + moves:
        copy.wait_send()


def shards(atmos_flux, weight_tiles, source_row, target_code, live_count):
    fields, rows, width = atmos_flux.shape
    cap = weight_tiles.shape[2]
    bands, subs = lax.axis_size("band"), lax.axis_size("sub")
    targets = 2 * subs * OB_DEV
    pieces = subs

    table = (-(-(1 + -(-targets // 128)) // 8) * 8, 128)
    block = (OB_DEV, fields, width)
    return pl.pallas_call(
        functools.partial(kernel, (fields, rows, width, cap, bands, subs)),
        out_shape=jax.ShapeDtypeStruct((fields, OB_DEV * width), jnp.float32),
        in_specs=[
            pl.BlockSpec(memory_space=pltpu.SMEM),
            pl.BlockSpec(memory_space=pltpu.SMEM),
            pl.BlockSpec(memory_space=pltpu.SMEM),
            pl.BlockSpec(memory_space=pltpu.HBM),
            pl.BlockSpec(memory_space=pltpu.HBM),
        ],
        out_specs=pl.BlockSpec(memory_space=pltpu.VMEM),
        scratch_shapes=[
            pltpu.VMEM(table, jnp.int32),
            pltpu.SMEM(table, jnp.int32),
            pltpu.VMEM((fields * rows, width), jnp.bfloat16),
            pltpu.VMEM((fields * rows, width), jnp.float32),
            pltpu.VMEM((rows, fields, 3 * width), jnp.bfloat16),
            pltpu.VMEM((cap, 3 * width, width), jnp.bfloat16),
            pltpu.VMEM((cap + 1, fields, width), jnp.float32),
            pltpu.VMEM((4, fields, width), jnp.bfloat16),
            pltpu.VMEM((4, fields, width), jnp.bfloat16),
            pltpu.VMEM((pieces,) + block, jnp.bfloat16),
            pltpu.VMEM((pieces,) + block, jnp.bfloat16),
            pltpu.VMEM((pieces - 1,) + block, jnp.bfloat16),
            pltpu.VMEM((pieces - 1,) + block, jnp.bfloat16),
            pltpu.SemaphoreType.DMA((5,)),
            pltpu.SemaphoreType.DMA((4,)),
            pltpu.SemaphoreType.DMA((4,)),
            pltpu.SemaphoreType.DMA((pieces,)),
            pltpu.SemaphoreType.DMA((pieces,)),
            pltpu.SemaphoreType.DMA((pieces - 1,)),
            pltpu.SemaphoreType.DMA((pieces - 1,)),
        ],
        compiler_params=pltpu.CompilerParams(
            collective_id=0, has_side_effects=True, vmem_limit_bytes=60 * 1024 * 1024
        ),
    )(source_row[0, 0], target_code[0, 0], live_count, atmos_flux.reshape(fields * rows, width), weight_tiles[0, 0])


def solution(mesh):
    return jax.shard_map(
        shards,
        mesh=mesh,
        in_specs=(
            P(None, "band", "sub"),
            P("band", "sub", None, None, None),
            P("band", "sub", None),
            P("band", "sub", None),
            P("band", "sub"),
        ),
        out_specs=P(None, ("band", "sub")),
        check_vma=False,
    )
```

```python
import functools

import jax
import jax.numpy as jnp
from jax import lax
from jax.experimental import pallas as pl
from jax.experimental.pallas import tpu as pltpu
from jax.sharding import PartitionSpec as P

OB_DEV = 8
MESH = pl.DeviceIdType.MESH


def kernel(
    sizes, row_ref, code_ref, live_ref, flux_ref, weight_ref, out_ref,
    table, found, xin, x32, op, wv, prefix, halo_out, halo_in, a_out, a_in, b_out, b_in,
    in_sem, halo_send, halo_recv, a_send, a_recv, b_send, b_recv,
):
    fields, rows, width, cap, bands, subs = sizes
    ny = subs // 2
    b = lax.axis_index("band")
    s = lax.axis_index("sub")
    y, core = s // 2, s % 2
    up, down = (b + 1) % bands, (b + bands - 1) % bands

    copy_flux = pltpu.make_async_copy(flux_ref, xin, in_sem.at[0])
    copy_flux.start()
    copy_w0 = pltpu.make_async_copy(weight_ref.at[:, :width], wv.at[:, :width], in_sem.at[1])
    copy_w0.start()
    half = cap // 2
    copy_w = []
    for part in range(2):
        where = (pl.ds(part * half, half), pl.ds(width, 2 * width))
        copy_w.append(pltpu.make_async_copy(weight_ref.at[where], wv.at[where], in_sem.at[2 + part]))
        copy_w[-1].start()

    barrier = pltpu.get_barrier_semaphore()
    for other in range(1, subs):
        pl.semaphore_signal(barrier, inc=1, device_id=(b, (s + other) % subs), device_id_type=MESH)
    for other in range(ny):
        pl.semaphore_signal(barrier, inc=1, device_id=(up, other * 2 + core), device_id_type=MESH)
        pl.semaphore_signal(barrier, inc=1, device_id=(down, other * 2 + core), device_id_type=MESH)

    part_row = lax.broadcasted_iota(jnp.int32, table.shape, 0)
    part_lane = lax.broadcasted_iota(jnp.int32, table.shape, 1)
    wanted = jnp.where(part_lane < 2 * OB_DEV, (part_row - 1) * 2 * OB_DEV + part_lane, -1)
    for e in range(cap):
        wanted = jnp.where((part_row == 0) & (part_lane == e), code_ref[e], wanted)
    limit = jnp.where(part_row == 0, part_lane, live_ref[0, 0])
    entry = jnp.full(table.shape, cap, jnp.int32)
    for e in range(cap):
        entry = jnp.where((wanted == code_ref[e]) & (limit > e), e, entry)
    table[...] = entry
    copy_found = pltpu.make_async_copy(table, found, in_sem.at[4])
    copy_found.start()

    copy_flux.wait()
    x32[...] = xin[...].astype(jnp.float32)
    lane = lax.broadcasted_iota(jnp.int32, (fields, width), 1)

    def row(i):
        return x32[pl.ds(i, fields, stride=rows), :]

    first = jnp.zeros((fields, width), jnp.float32)
    last = jnp.zeros((fields, width), jnp.float32)
    for i in range(rows):
        x = row(i)
        op[i, :, :width] = x.astype(jnp.bfloat16)
        first = jnp.where(lane == i, x[:, :1], first)
        last = jnp.where(lane == i, x[:, width - 1:], last)
    halo_out[0] = row(rows - 1).astype(jnp.bfloat16)
    halo_out[1] = row(0).astype(jnp.bfloat16)
    halo_out[2] = last.astype(jnp.bfloat16)
    halo_out[3] = first.astype(jnp.bfloat16)
    prefix[cap] = jnp.zeros((fields, width), jnp.float32)

    pl.semaphore_wait(barrier, subs - 1 + 2 * ny)

    partners = ((up, s), (down, s), (b, (s + 1) % subs), (b, (s + subs - 1) % subs))
    sends = (b < bands - 1, b > 0, s < subs - 1, s > 0)
    receives = (b > 0, b < bands - 1, s > 0, s < subs - 1)
    halos = [
        pltpu.make_async_remote_copy(
            src_ref=halo_out.at[k], dst_ref=halo_in.at[k], send_sem=halo_send.at[k], recv_sem=halo_recv.at[k],
            device_id=partners[k], device_id_type=MESH)
        for k in range(4)
    ]
    for k in range(4):
        @pl.when(sends[k])
        def _(k=k):
            halos[k].start()

    copy_w0.wait()

    def flux_part(e, carry):
        picked = op[row_ref[e], :, :width]
        prefix[e] = jnp.dot(picked, wv[e, :width], preferred_element_type=jnp.float32)
        return carry

    lax.fori_loop(0, cap, flux_part, 0, unroll=True)

    for k in range(4):
        @pl.when(receives[k])
        def _(k=k):
            halos[k].wait_recv()

        @pl.when(jnp.logical_not(receives[k]))
        def _(k=k):
            halo_in[k] = jnp.zeros((fields, width), jnp.bfloat16)

    below, above, left, right = (halo_in[k].astype(jnp.float32) for k in range(4))
    for i in range(rows):
        x = row(i)
        before = row(i - 1) if i > 0 else below
        after = row(i + 1) if i < rows - 1 else above
        west = jnp.where(lane == 0, left[:, i:i + 1], pltpu.roll(x, 1, 1))
        east = jnp.where(lane == width - 1, right[:, i:i + 1], pltpu.roll(x, width - 1, 1))
        op[i, :, width:2 * width] = (0.5 * (east - west)).astype(jnp.bfloat16)
        op[i, :, 2 * width:] = (0.5 * (after - before)).astype(jnp.bfloat16)

    def gradient_part(e, carry):
        picked = op[row_ref[e], :, width:]
        product = jnp.dot(picked, wv[e, width:], preferred_element_type=jnp.float32)
        prefix[e] = prefix[e] + product
        return carry

    def chain(e, carry):
        prefix[e] = prefix[e] + prefix[found[0, e]]
        return carry

    for part in range(2):
        copy_w[part].wait()
        lax.fori_loop(part * half, (part + 1) * half, gradient_part, 0, unroll=True)
    copy_found.wait()
    lax.fori_loop(0, cap, chain, 0, unroll=True)

    def partial(sub, step, q):
        return prefix[found[1 + sub, step * OB_DEV + q]]

    pieces = [(j, 1) for j in range(1, ny)] + [(0, 1)] + [(j, 0) for j in range(1, ny)] + [(0, 0)]
    swaps, moves = [], []
    for p, (j, step) in enumerate(pieces):
        target = (y + j) % ny * 2 + 1 - core
        for q in range(OB_DEV):
            a_out[p, q] = partial(target, step, q).astype(jnp.bfloat16)
        swaps.append(pltpu.make_async_remote_copy(
            src_ref=a_out.at[p], dst_ref=a_in.at[p], send_sem=a_send.at[p], recv_sem=a_recv.at[p],
            device_id=(b, y * 2 + 1 - core), device_id_type=MESH))
        swaps[-1].start()
    for p, (j, step) in enumerate(pieces):
        target = (y + j) % ny * 2 + core
        swaps[p].wait_recv()
        if (j, step) == (0, 0):
            for q in range(OB_DEV):
                out_ref[:, q * width:(q + 1) * width] = partial(target, step, q) + a_in[p, q].astype(jnp.float32)
            continue
        for q in range(OB_DEV):
            b_out[p, q] = (partial(target, step, q) + a_in[p, q].astype(jnp.float32)).astype(jnp.bfloat16)
        moves.append(pltpu.make_async_remote_copy(
            src_ref=b_out.at[p], dst_ref=b_in.at[p], send_sem=b_send.at[p], recv_sem=b_recv.at[p],
            device_id=(up if step else b, target), device_id_type=MESH))
        moves[-1].start()
    for p, move in enumerate(moves):
        move.wait_recv()
        for q in range(OB_DEV):
            out_ref[:, q * width:(q + 1) * width] += b_in[p, q].astype(jnp.float32)

    for k in range(4):
        @pl.when(sends[k])
        def _(k=k):
            halos[k].wait_send()
    for copy in swaps + moves:
        copy.wait_send()


def shards(atmos_flux, weight_tiles, source_row, target_code, live_count):
    fields, rows, width = atmos_flux.shape
    cap = weight_tiles.shape[2]
    bands, subs = lax.axis_size("band"), lax.axis_size("sub")
    pieces = subs

    table = (-(-(1 + subs) // 8) * 8, 128)
    block = (OB_DEV, fields, width)
    return pl.pallas_call(
        functools.partial(kernel, (fields, rows, width, cap, bands, subs)),
        out_shape=pltpu.VMEM((fields, OB_DEV * width), jnp.float32),
        in_specs=[
            pl.BlockSpec(memory_space=pltpu.SMEM),
            pl.BlockSpec(memory_space=pltpu.SMEM),
            pl.BlockSpec(memory_space=pltpu.SMEM),
            pl.BlockSpec(memory_space=pltpu.HBM),
            pl.BlockSpec(memory_space=pltpu.HBM),
        ],
        out_specs=pl.BlockSpec(memory_space=pltpu.VMEM),
        scratch_shapes=[
            pltpu.VMEM(table, jnp.int32),
            pltpu.SMEM(table, jnp.int32),
            pltpu.VMEM((fields * rows, width), jnp.bfloat16),
            pltpu.VMEM((fields * rows, width), jnp.float32),
            pltpu.VMEM((rows, fields, 3 * width), jnp.bfloat16),
            pltpu.VMEM((cap, 3 * width, width), jnp.bfloat16),
            pltpu.VMEM((cap + 1, fields, width), jnp.float32),
            pltpu.VMEM((4, fields, width), jnp.bfloat16),
            pltpu.VMEM((4, fields, width), jnp.bfloat16),
            pltpu.VMEM((pieces,) + block, jnp.bfloat16),
            pltpu.VMEM((pieces,) + block, jnp.bfloat16),
            pltpu.VMEM((pieces - 1,) + block, jnp.bfloat16),
            pltpu.VMEM((pieces - 1,) + block, jnp.bfloat16),
            pltpu.SemaphoreType.DMA((5,)),
            pltpu.SemaphoreType.DMA((4,)),
            pltpu.SemaphoreType.DMA((4,)),
            pltpu.SemaphoreType.DMA((pieces,)),
            pltpu.SemaphoreType.DMA((pieces,)),
            pltpu.SemaphoreType.DMA((pieces - 1,)),
            pltpu.SemaphoreType.DMA((pieces - 1,)),
        ],
        compiler_params=pltpu.CompilerParams(
            collective_id=0, has_side_effects=True, vmem_limit_bytes=60 * 1024 * 1024
        ),
    )(source_row[0, 0], target_code[0, 0], live_count, atmos_flux.reshape(fields * rows, width), weight_tiles[0, 0])


def solution(mesh):
    return jax.shard_map(
        shards,
        mesh=mesh,
        in_specs=(
            P(None, "band", "sub"),
            P("band", "sub", None, None, None),
            P("band", "sub", None),
            P("band", "sub", None),
            P("band", "sub"),
        ),
        out_specs=P(None, ("band", "sub")),
        check_vma=False,
    )
```

```python
import functools

import jax
import jax.numpy as jnp
from jax import lax
from jax.experimental import pallas as pl
from jax.experimental.pallas import tpu as pltpu
from jax.sharding import PartitionSpec as P

OB_DEV = 8
MESH = pl.DeviceIdType.MESH


def kernel(
    sizes, row_hbm, code_hbm, live_ref, flux_ref, weight_ref, out_ref,
    row_ref, code_ref, table, found, xin, x32, op, wv, prefix, halo_out, halo_in, a_out, a_in, b_out, b_in,
    in_sem, halo_send, halo_recv, a_send, a_recv, b_send, b_recv,
):
    fields, rows, width, cap, bands, subs = sizes
    ny = subs // 2
    b = lax.axis_index("band")
    s = lax.axis_index("sub")
    y, core = s // 2, s % 2
    up, down = (b + 1) % bands, (b + bands - 1) % bands

    barrier = pltpu.get_barrier_semaphore()
    for other in range(1, subs):
        pl.semaphore_signal(barrier, inc=1, device_id=(b, (s + other) % subs), device_id_type=MESH)
    for other in range(ny):
        pl.semaphore_signal(barrier, inc=1, device_id=(up, other * 2 + core), device_id_type=MESH)
        pl.semaphore_signal(barrier, inc=1, device_id=(down, other * 2 + core), device_id_type=MESH)

    copy_flux = pltpu.make_async_copy(flux_ref, xin, in_sem.at[0])
    copy_flux.start()
    small = []
    for k, (source, place) in enumerate(((code_hbm, code_ref), (row_hbm, row_ref))):
        small.append(pltpu.make_async_copy(source, place, in_sem.at[5 + k]))
        small[-1].start()
    copy_w0 = pltpu.make_async_copy(weight_ref.at[:, :width], wv.at[:, :width], in_sem.at[1])
    copy_w0.start()
    half = cap // 2
    copy_w = []
    for part in range(2):
        where = (pl.ds(part * half, half), pl.ds(width, 2 * width))
        copy_w.append(pltpu.make_async_copy(weight_ref.at[where], wv.at[where], in_sem.at[2 + part]))
        copy_w[-1].start()

    copy_flux.wait()
    x32[...] = xin[...].astype(jnp.float32)
    lane = lax.broadcasted_iota(jnp.int32, (fields, width), 1)

    def row(i):
        return x32[pl.ds(i, fields, stride=rows), :]

    first = jnp.zeros((fields, width), jnp.float32)
    last = jnp.zeros((fields, width), jnp.float32)
    for i in range(rows):
        x = row(i)
        first = jnp.where(lane == i, x[:, :1], first)
        last = jnp.where(lane == i, x[:, width - 1:], last)
    halo_out[0] = row(rows - 1).astype(jnp.bfloat16)
    halo_out[1] = row(0).astype(jnp.bfloat16)
    halo_out[2] = last.astype(jnp.bfloat16)
    halo_out[3] = first.astype(jnp.bfloat16)

    pl.semaphore_wait(barrier, subs - 1 + 2 * ny)

    partners = ((up, s), (down, s), (b, (s + 1) % subs), (b, (s + subs - 1) % subs))
    sends = (b < bands - 1, b > 0, s < subs - 1, s > 0)
    receives = (b > 0, b < bands - 1, s > 0, s < subs - 1)
    halos = [
        pltpu.make_async_remote_copy(
            src_ref=halo_out.at[k], dst_ref=halo_in.at[k], send_sem=halo_send.at[k], recv_sem=halo_recv.at[k],
            device_id=partners[k], device_id_type=MESH)
        for k in range(4)
    ]
    for k in range(4):
        @pl.when(sends[k])
        def _(k=k):
            halos[k].start()

    for copy in small:
        copy.wait()
    part_row = lax.broadcasted_iota(jnp.int32, table.shape, 0)
    part_lane = lax.broadcasted_iota(jnp.int32, table.shape, 1)
    wanted = jnp.where(part_lane < 2 * OB_DEV, (part_row - 1) * 2 * OB_DEV + part_lane, -1)
    for e in range(cap):
        wanted = jnp.where((part_row == 0) & (part_lane == e), code_ref[e], wanted)
    limit = jnp.where(part_row == 0, part_lane, live_ref[0, 0])
    entry = jnp.full(table.shape, cap, jnp.int32)
    for e in range(cap):
        entry = jnp.where((wanted == code_ref[e]) & (limit > e), e, entry)
    table[...] = entry
    copy_found = pltpu.make_async_copy(table, found, in_sem.at[4])
    copy_found.start()

    for i in range(rows):
        op[i, :, :width] = row(i).astype(jnp.bfloat16)
    prefix[cap] = jnp.zeros((fields, width), jnp.float32)
    copy_w0.wait()

    def flux_part(e, carry):
        picked = op[row_ref[e], :, :width]
        prefix[e] = jnp.dot(picked, wv[e, :width], preferred_element_type=jnp.float32)
        return carry

    lax.fori_loop(0, cap, flux_part, 0, unroll=True)

    for k in range(4):
        @pl.when(receives[k])
        def _(k=k):
            halos[k].wait_recv()

        @pl.when(jnp.logical_not(receives[k]))
        def _(k=k):
            halo_in[k] = jnp.zeros((fields, width), jnp.bfloat16)

    below, above, left, right = (halo_in[k].astype(jnp.float32) for k in range(4))
    for i in range(rows):
        x = row(i)
        before = row(i - 1) if i > 0 else below
        after = row(i + 1) if i < rows - 1 else above
        west = jnp.where(lane == 0, left[:, i:i + 1], pltpu.roll(x, 1, 1))
        east = jnp.where(lane == width - 1, right[:, i:i + 1], pltpu.roll(x, width - 1, 1))
        op[i, :, width:2 * width] = (0.5 * (east - west)).astype(jnp.bfloat16)
        op[i, :, 2 * width:] = (0.5 * (after - before)).astype(jnp.bfloat16)

    def gradient_part(e, carry):
        picked = op[row_ref[e], :, width:]
        product = jnp.dot(picked, wv[e, width:], preferred_element_type=jnp.float32)
        prefix[e] = prefix[e] + product
        return carry

    def chain(e, carry):
        prefix[e] = prefix[e] + prefix[found[0, e]]
        return carry

    for part in range(2):
        copy_w[part].wait()
        lax.fori_loop(part * half, (part + 1) * half, gradient_part, 0, unroll=True)
    copy_found.wait()
    lax.fori_loop(0, cap, chain, 0, unroll=True)

    def partial(sub, step, q):
        return prefix[found[1 + sub, step * OB_DEV + q]]

    pieces = [(j, 1) for j in range(1, ny)] + [(0, 1)] + [(j, 0) for j in range(1, ny)] + [(0, 0)]
    swaps, moves = [], []
    for p, (j, step) in enumerate(pieces):
        target = (y + j) % ny * 2 + 1 - core
        for q in range(OB_DEV):
            a_out[p, q] = partial(target, step, q).astype(jnp.bfloat16)
        swaps.append(pltpu.make_async_remote_copy(
            src_ref=a_out.at[p], dst_ref=a_in.at[p], send_sem=a_send.at[p], recv_sem=a_recv.at[p],
            device_id=(b, y * 2 + 1 - core), device_id_type=MESH))
        swaps[-1].start()
    for p, (j, step) in enumerate(pieces):
        target = (y + j) % ny * 2 + core
        swaps[p].wait_recv()
        if (j, step) == (0, 0):
            for q in range(OB_DEV):
                out_ref[:, q * width:(q + 1) * width] = partial(target, step, q) + a_in[p, q].astype(jnp.float32)
            continue
        for q in range(OB_DEV):
            b_out[p, q] = (partial(target, step, q) + a_in[p, q].astype(jnp.float32)).astype(jnp.bfloat16)
        moves.append(pltpu.make_async_remote_copy(
            src_ref=b_out.at[p], dst_ref=b_in.at[p], send_sem=b_send.at[p], recv_sem=b_recv.at[p],
            device_id=(up if step else b, target), device_id_type=MESH))
        moves[-1].start()
    for p, move in enumerate(moves):
        move.wait_recv()
        for q in range(OB_DEV):
            out_ref[:, q * width:(q + 1) * width] += b_in[p, q].astype(jnp.float32)

    for k in range(4):
        @pl.when(sends[k])
        def _(k=k):
            halos[k].wait_send()
    for copy in swaps + moves:
        copy.wait_send()


def shards(atmos_flux, weight_tiles, source_row, target_code, live_count):
    fields, rows, width = atmos_flux.shape
    cap = weight_tiles.shape[2]
    bands, subs = lax.axis_size("band"), lax.axis_size("sub")
    pieces = subs

    table = (-(-(1 + subs) // 8) * 8, 128)
    block = (OB_DEV, fields, width)
    return pl.pallas_call(
        functools.partial(kernel, (fields, rows, width, cap, bands, subs)),
        out_shape=pltpu.VMEM((fields, OB_DEV * width), jnp.float32),
        in_specs=[
            pl.BlockSpec(memory_space=pltpu.HBM),
            pl.BlockSpec(memory_space=pltpu.HBM),
            pl.BlockSpec(memory_space=pltpu.SMEM),
            pl.BlockSpec(memory_space=pltpu.HBM),
            pl.BlockSpec(memory_space=pltpu.HBM),
        ],
        out_specs=pl.BlockSpec(memory_space=pltpu.VMEM),
        scratch_shapes=[
            pltpu.SMEM((cap,), jnp.int32),
            pltpu.SMEM((cap,), jnp.int32),
            pltpu.VMEM(table, jnp.int32),
            pltpu.SMEM(table, jnp.int32),
            pltpu.VMEM((fields * rows, width), jnp.bfloat16),
            pltpu.VMEM((fields * rows, width), jnp.float32),
            pltpu.VMEM((rows, fields, 3 * width), jnp.bfloat16),
            pltpu.VMEM((cap, 3 * width, width), jnp.bfloat16),
            pltpu.VMEM((cap + 1, fields, width), jnp.float32),
            pltpu.VMEM((4, fields, width), jnp.bfloat16),
            pltpu.VMEM((4, fields, width), jnp.bfloat16),
            pltpu.VMEM((pieces,) + block, jnp.bfloat16),
            pltpu.VMEM((pieces,) + block, jnp.bfloat16),
            pltpu.VMEM((pieces - 1,) + block, jnp.bfloat16),
            pltpu.VMEM((pieces - 1,) + block, jnp.bfloat16),
            pltpu.SemaphoreType.DMA((7,)),
            pltpu.SemaphoreType.DMA((4,)),
            pltpu.SemaphoreType.DMA((4,)),
            pltpu.SemaphoreType.DMA((pieces,)),
            pltpu.SemaphoreType.DMA((pieces,)),
            pltpu.SemaphoreType.DMA((pieces - 1,)),
            pltpu.SemaphoreType.DMA((pieces - 1,)),
        ],
        compiler_params=pltpu.CompilerParams(
            collective_id=0, has_side_effects=True, vmem_limit_bytes=60 * 1024 * 1024
        ),
    )(source_row[0, 0], target_code[0, 0], live_count, atmos_flux.reshape(fields * rows, width), weight_tiles[0, 0])


def solution(mesh):
    return jax.shard_map(
        shards,
        mesh=mesh,
        in_specs=(
            P(None, "band", "sub"),
            P("band", "sub", None, None, None),
            P("band", "sub", None),
            P("band", "sub", None),
            P("band", "sub"),
        ),
        out_specs=P(None, ("band", "sub")),
        check_vma=False,
    )
```

```python
import functools

import jax
import jax.numpy as jnp
from jax import lax
from jax.experimental import pallas as pl
from jax.experimental.pallas import tpu as pltpu
from jax.sharding import PartitionSpec as P

OB_DEV = 8
MESH = pl.DeviceIdType.MESH


def kernel(
    sizes, row_hbm, code_hbm, live_ref, flux_ref, weight_ref, out_ref,
    row_ref, code_ref, table, found, xin, x32, op, wv, prefix, halo_out, halo_in, a_out, a_in, b_out, b_in,
    in_sem, halo_send, halo_recv, a_send, a_recv, b_send, b_recv,
):
    fields, rows, width, cap, bands, subs = sizes
    ny = subs // 2
    b = lax.axis_index("band")
    s = lax.axis_index("sub")
    y, core = s // 2, s % 2
    up, down = (b + 1) % bands, (b + bands - 1) % bands

    barrier = pltpu.get_barrier_semaphore()
    for other in range(1, subs):
        pl.semaphore_signal(barrier, inc=1, device_id=(b, (s + other) % subs), device_id_type=MESH)
    for other in range(ny):
        pl.semaphore_signal(barrier, inc=1, device_id=(up, other * 2 + core), device_id_type=MESH)
        pl.semaphore_signal(barrier, inc=1, device_id=(down, other * 2 + core), device_id_type=MESH)

    copy_flux = pltpu.make_async_copy(flux_ref, xin, in_sem.at[0])
    copy_flux.start()
    small = []
    for k, (source, place) in enumerate(((code_hbm, code_ref), (row_hbm, row_ref))):
        small.append(pltpu.make_async_copy(source, place, in_sem.at[5 + k]))
        small[-1].start()
    copy_w0 = pltpu.make_async_copy(weight_ref.at[:, :width], wv.at[:, :width], in_sem.at[1])
    copy_w0.start()
    half = cap // 2
    copy_w = []
    for part in range(2):
        where = (pl.ds(part * half, half), pl.ds(width, 2 * width))
        copy_w.append(pltpu.make_async_copy(weight_ref.at[where], wv.at[where], in_sem.at[2 + part]))
        copy_w[-1].start()

    copy_flux.wait()
    x32[...] = xin[...].astype(jnp.float32)
    lane = lax.broadcasted_iota(jnp.int32, (fields, width), 1)

    def row(i):
        return x32[pl.ds(i, fields, stride=rows), :]

    first = jnp.zeros((fields, width), jnp.float32)
    last = jnp.zeros((fields, width), jnp.float32)
    for i in range(rows):
        x = row(i)
        first = jnp.where(lane == i, x[:, :1], first)
        last = jnp.where(lane == i, x[:, width - 1:], last)
    halo_out[0] = row(rows - 1).astype(jnp.bfloat16)
    halo_out[1] = row(0).astype(jnp.bfloat16)
    halo_out[2] = last.astype(jnp.bfloat16)
    halo_out[3] = first.astype(jnp.bfloat16)

    pl.semaphore_wait(barrier, subs - 1 + 2 * ny)

    partners = ((up, s), (down, s), (b, (s + 1) % subs), (b, (s + subs - 1) % subs))
    sends = (b < bands - 1, b > 0, s < subs - 1, s > 0)
    receives = (b > 0, b < bands - 1, s > 0, s < subs - 1)
    halos = [
        pltpu.make_async_remote_copy(
            src_ref=halo_out.at[k], dst_ref=halo_in.at[k], send_sem=halo_send.at[k], recv_sem=halo_recv.at[k],
            device_id=partners[k], device_id_type=MESH)
        for k in range(4)
    ]
    for k in range(4):
        @pl.when(sends[k])
        def _(k=k):
            halos[k].start()

    for copy in small:
        copy.wait()
    part_row = lax.broadcasted_iota(jnp.int32, table.shape, 0)
    part_lane = lax.broadcasted_iota(jnp.int32, table.shape, 1)
    wanted = jnp.where(part_lane < 2 * OB_DEV, (part_row - 1) * 2 * OB_DEV + part_lane, -1)
    for e in range(cap):
        wanted = jnp.where((part_row == 0) & (part_lane == e), code_ref[e], wanted)
    limit = jnp.where(part_row == 0, part_lane, live_ref[0, 0])
    entry = jnp.full(table.shape, cap, jnp.int32)
    for e in range(cap):
        entry = jnp.where((wanted == code_ref[e]) & (limit > e), e, entry)
    table[...] = entry
    copy_found = pltpu.make_async_copy(table, found, in_sem.at[4])
    copy_found.start()

    for i in range(rows):
        op[i, :, :width] = row(i).astype(jnp.bfloat16)
    prefix[cap] = jnp.zeros((fields, width), jnp.float32)
    copy_w0.wait()

    def flux_part(e, carry):
        picked = op[row_ref[e], :, :width]
        prefix[e] = jnp.dot(picked, wv[e, :width], preferred_element_type=jnp.float32)
        return carry

    lax.fori_loop(0, cap, flux_part, 0, unroll=8)

    for k in range(4):
        @pl.when(receives[k])
        def _(k=k):
            halos[k].wait_recv()

        @pl.when(jnp.logical_not(receives[k]))
        def _(k=k):
            halo_in[k] = jnp.zeros((fields, width), jnp.bfloat16)

    below, above, left, right = (halo_in[k].astype(jnp.float32) for k in range(4))
    for i in range(rows):
        x = row(i)
        before = row(i - 1) if i > 0 else below
        after = row(i + 1) if i < rows - 1 else above
        west = jnp.where(lane == 0, left[:, i:i + 1], pltpu.roll(x, 1, 1))
        east = jnp.where(lane == width - 1, right[:, i:i + 1], pltpu.roll(x, width - 1, 1))
        op[i, :, width:2 * width] = (0.5 * (east - west)).astype(jnp.bfloat16)
        op[i, :, 2 * width:] = (0.5 * (after - before)).astype(jnp.bfloat16)

    def gradient_part(e, carry):
        picked = op[row_ref[e], :, width:]
        product = jnp.dot(picked, wv[e, width:], preferred_element_type=jnp.float32)
        prefix[e] = prefix[e] + product
        return carry

    def chain(e, carry):
        prefix[e] = prefix[e] + prefix[found[0, e]]
        return carry

    for part in range(2):
        copy_w[part].wait()
    lax.fori_loop(0, cap, gradient_part, 0, unroll=16)
    copy_found.wait()
    lax.fori_loop(0, cap, chain, 0, unroll=8)

    def partial(sub, step, q):
        return prefix[found[1 + sub, step * OB_DEV + q]]

    pieces = [(j, 1) for j in range(1, ny)] + [(0, 1)] + [(j, 0) for j in range(1, ny)] + [(0, 0)]
    swaps, moves = [], []

    def swap(p):
        j, step = pieces[p]
        target = (y + j) % ny * 2 + 1 - core
        for q in range(OB_DEV):
            a_out[p, q] = partial(target, step, q).astype(jnp.bfloat16)
        swaps.append(pltpu.make_async_remote_copy(
            src_ref=a_out.at[p], dst_ref=a_in.at[p], send_sem=a_send.at[p], recv_sem=a_recv.at[p],
            device_id=(b, y * 2 + 1 - core), device_id_type=MESH))
        swaps[-1].start()

    def move(p):
        j, step = pieces[p]
        target = (y + j) % ny * 2 + core
        swaps[p].wait_recv()
        if (j, step) == (0, 0):
            for q in range(OB_DEV):
                out_ref[:, q * width:(q + 1) * width] = partial(target, step, q) + a_in[p, q].astype(jnp.float32)
            return
        for q in range(OB_DEV):
            b_out[p, q] = (partial(target, step, q) + a_in[p, q].astype(jnp.float32)).astype(jnp.bfloat16)
        moves.append(pltpu.make_async_remote_copy(
            src_ref=b_out.at[p], dst_ref=b_in.at[p], send_sem=b_send.at[p], recv_sem=b_recv.at[p],
            device_id=(up if step else b, target), device_id_type=MESH))
        moves[-1].start()

    ahead = ny
    for p in range(ahead):
        swap(p)
    for p in range(len(pieces)):
        move(p)
        if p + ahead < len(pieces):
            swap(p + ahead)
    for p, arrival in enumerate(moves):
        arrival.wait_recv()
        for q in range(OB_DEV):
            out_ref[:, q * width:(q + 1) * width] += b_in[p, q].astype(jnp.float32)

    for k in range(4):
        @pl.when(sends[k])
        def _(k=k):
            halos[k].wait_send()
    for copy in swaps + moves:
        copy.wait_send()


def shards(atmos_flux, weight_tiles, source_row, target_code, live_count):
    fields, rows, width = atmos_flux.shape
    cap = weight_tiles.shape[2]
    bands, subs = lax.axis_size("band"), lax.axis_size("sub")
    pieces = subs

    table = (-(-(1 + subs) // 8) * 8, 128)
    block = (OB_DEV, fields, width)
    return pl.pallas_call(
        functools.partial(kernel, (fields, rows, width, cap, bands, subs)),
        out_shape=pltpu.VMEM((fields, OB_DEV * width), jnp.float32),
        in_specs=[
            pl.BlockSpec(memory_space=pltpu.HBM),
            pl.BlockSpec(memory_space=pltpu.HBM),
            pl.BlockSpec(memory_space=pltpu.SMEM),
            pl.BlockSpec(memory_space=pltpu.HBM),
            pl.BlockSpec(memory_space=pltpu.HBM),
        ],
        out_specs=pl.BlockSpec(memory_space=pltpu.VMEM),
        scratch_shapes=[
            pltpu.SMEM((cap,), jnp.int32),
            pltpu.SMEM((cap,), jnp.int32),
            pltpu.VMEM(table, jnp.int32),
            pltpu.SMEM(table, jnp.int32),
            pltpu.VMEM((fields * rows, width), jnp.bfloat16),
            pltpu.VMEM((fields * rows, width), jnp.float32),
            pltpu.VMEM((rows, fields, 3 * width), jnp.bfloat16),
            pltpu.VMEM((cap, 3 * width, width), jnp.bfloat16),
            pltpu.VMEM((cap + 1, fields, width), jnp.float32),
            pltpu.VMEM((4, fields, width), jnp.bfloat16),
            pltpu.VMEM((4, fields, width), jnp.bfloat16),
            pltpu.VMEM((pieces,) + block, jnp.bfloat16),
            pltpu.VMEM((pieces,) + block, jnp.bfloat16),
            pltpu.VMEM((pieces - 1,) + block, jnp.bfloat16),
            pltpu.VMEM((pieces - 1,) + block, jnp.bfloat16),
            pltpu.SemaphoreType.DMA((7,)),
            pltpu.SemaphoreType.DMA((4,)),
            pltpu.SemaphoreType.DMA((4,)),
            pltpu.SemaphoreType.DMA((pieces,)),
            pltpu.SemaphoreType.DMA((pieces,)),
            pltpu.SemaphoreType.DMA((pieces - 1,)),
            pltpu.SemaphoreType.DMA((pieces - 1,)),
        ],
        compiler_params=pltpu.CompilerParams(
            collective_id=0, has_side_effects=True, vmem_limit_bytes=60 * 1024 * 1024
        ),
    )(source_row[0, 0], target_code[0, 0], live_count, atmos_flux.reshape(fields * rows, width), weight_tiles[0, 0])


def solution(mesh):
    return jax.shard_map(
        shards,
        mesh=mesh,
        in_specs=(
            P(None, "band", "sub"),
            P("band", "sub", None, None, None),
            P("band", "sub", None),
            P("band", "sub", None),
            P("band", "sub"),
        ),
        out_specs=P(None, ("band", "sub")),
        check_vma=False,
    )
```

```python
import functools

import jax
import jax.numpy as jnp
from jax import lax
from jax.experimental import pallas as pl
from jax.experimental.pallas import tpu as pltpu
from jax.sharding import PartitionSpec as P

OB_DEV = 8
MESH = pl.DeviceIdType.MESH


def kernel(
    sizes, row_hbm, code_hbm, live_ref, flux_ref, weight_ref, out_ref,
    row_ref, code_ref, table, found, xin, x32, dx, op, wv, prefix, halo_out, halo_in, a_out, a_in, b_out, b_in,
    in_sem, halo_send, halo_recv, a_send, a_recv, b_send, b_recv,
):
    fields, rows, width, cap, bands, subs = sizes
    ny = subs // 2
    b = lax.axis_index("band")
    s = lax.axis_index("sub")
    y, core = s // 2, s % 2
    up, down = (b + 1) % bands, (b + bands - 1) % bands

    barrier = pltpu.get_barrier_semaphore()
    for other in range(1, subs):
        pl.semaphore_signal(barrier, inc=1, device_id=(b, (s + other) % subs), device_id_type=MESH)
    for other in range(ny):
        pl.semaphore_signal(barrier, inc=1, device_id=(up, other * 2 + core), device_id_type=MESH)
        pl.semaphore_signal(barrier, inc=1, device_id=(down, other * 2 + core), device_id_type=MESH)

    copy_flux = pltpu.make_async_copy(flux_ref, xin, in_sem.at[0])
    copy_flux.start()
    small = []
    for k, (source, place) in enumerate(((code_hbm, code_ref), (row_hbm, row_ref))):
        small.append(pltpu.make_async_copy(source, place, in_sem.at[5 + k]))
        small[-1].start()
    copy_w0 = pltpu.make_async_copy(weight_ref.at[:, :width], wv.at[:, :width], in_sem.at[1])
    copy_w0.start()
    half = cap // 2
    copy_w = []
    for part in range(2):
        where = (pl.ds(part * half, half), pl.ds(width, 2 * width))
        copy_w.append(pltpu.make_async_copy(weight_ref.at[where], wv.at[where], in_sem.at[2 + part]))
        copy_w[-1].start()

    copy_flux.wait()
    x32[...] = xin[...].astype(jnp.float32)
    lane = lax.broadcasted_iota(jnp.int32, (fields, width), 1)

    def row(i):
        return x32[pl.ds(i, fields, stride=rows), :]

    first = jnp.zeros((fields, width), jnp.float32)
    last = jnp.zeros((fields, width), jnp.float32)
    for i in range(rows):
        x = row(i)
        first = jnp.where(lane == i, x[:, :1], first)
        last = jnp.where(lane == i, x[:, width - 1:], last)
    halo_out[0] = row(rows - 1).astype(jnp.bfloat16)
    halo_out[1] = row(0).astype(jnp.bfloat16)
    halo_out[2] = last.astype(jnp.bfloat16)
    halo_out[3] = first.astype(jnp.bfloat16)

    pl.semaphore_wait(barrier, subs - 1 + 2 * ny)

    partners = ((up, s), (down, s), (b, (s + 1) % subs), (b, (s + subs - 1) % subs))
    sends = (b < bands - 1, b > 0, s < subs - 1, s > 0)
    receives = (b > 0, b < bands - 1, s > 0, s < subs - 1)
    halos = [
        pltpu.make_async_remote_copy(
            src_ref=halo_out.at[k], dst_ref=halo_in.at[k], send_sem=halo_send.at[k], recv_sem=halo_recv.at[k],
            device_id=partners[k], device_id_type=MESH)
        for k in range(4)
    ]
    for k in range(4):
        @pl.when(sends[k])
        def _(k=k):
            halos[k].start()

    for copy in small:
        copy.wait()
    part_row = lax.broadcasted_iota(jnp.int32, table.shape, 0)
    part_lane = lax.broadcasted_iota(jnp.int32, table.shape, 1)
    wanted = jnp.where(part_lane < 2 * OB_DEV, (part_row - 1) * 2 * OB_DEV + part_lane, -1)
    for e in range(cap):
        wanted = jnp.where((part_row == 0) & (part_lane == e), code_ref[e], wanted)
    limit = jnp.where(part_row == 0, part_lane, live_ref[0, 0])
    entry = jnp.full(table.shape, cap, jnp.int32)
    for e in range(cap):
        entry = jnp.where((wanted == code_ref[e]) & (limit > e), e, entry)
    table[...] = entry
    copy_found = pltpu.make_async_copy(table, found, in_sem.at[4])
    copy_found.start()

    for i in range(rows):
        x = row(i)
        op[i, :, :width] = x.astype(jnp.bfloat16)
        east = jnp.where(lane == width - 1, 0.0, pltpu.roll(x, width - 1, 1))
        west = jnp.where(lane == 0, 0.0, pltpu.roll(x, 1, 1))
        dx[i] = east - west
        if 0 < i < rows - 1:
            op[i, :, 2 * width:] = (0.5 * (row(i + 1) - row(i - 1))).astype(jnp.bfloat16)
    prefix[cap] = jnp.zeros((fields, width), jnp.float32)
    copy_w0.wait()

    def flux_part(e, carry):
        picked = op[row_ref[e], :, :width]
        prefix[e] = jnp.dot(picked, wv[e, :width], preferred_element_type=jnp.float32)
        return carry

    lax.fori_loop(0, cap, flux_part, 0, unroll=8)

    for k in range(4):
        @pl.when(receives[k])
        def _(k=k):
            halos[k].wait_recv()

        @pl.when(jnp.logical_not(receives[k]))
        def _(k=k):
            halo_in[k] = jnp.zeros((fields, width), jnp.bfloat16)

    below, above, left, right = (halo_in[k].astype(jnp.float32) for k in range(4))
    for i in range(rows):
        edge = jnp.where(lane == 0, -left[:, i:i + 1], jnp.where(lane == width - 1, right[:, i:i + 1], 0.0))
        op[i, :, width:2 * width] = (0.5 * (dx[i] + edge)).astype(jnp.bfloat16)
    op[0, :, 2 * width:] = (0.5 * (row(1) - below)).astype(jnp.bfloat16)
    op[rows - 1, :, 2 * width:] = (0.5 * (above - row(rows - 2))).astype(jnp.bfloat16)

    def gradient_part(e, carry):
        picked = op[row_ref[e], :, width:]
        product = jnp.dot(picked, wv[e, width:], preferred_element_type=jnp.float32)
        prefix[e] = prefix[e] + product
        return carry

    def chain(e, carry):
        prefix[e] = prefix[e] + prefix[found[0, e]]
        return carry

    for part in range(2):
        copy_w[part].wait()
    lax.fori_loop(0, cap, gradient_part, 0, unroll=16)
    copy_found.wait()
    lax.fori_loop(0, cap, chain, 0, unroll=8)

    def partial(sub, step, q):
        return prefix[found[1 + sub, step * OB_DEV + q]]

    away = [(j, 1) for j in range(1, ny)] + [(0, 1)] + [(j, 0) for j in range(1, ny)] + [(0, 0)]
    count = a_out.shape[1]
    cuts = OB_DEV // count
    pieces = [(j, step, cut * count) for j, step in away for cut in range(cuts)]
    swaps, moves = [], []

    def swap(p):
        j, step, lead = pieces[p]
        target = (y + j) % ny * 2 + 1 - core
        for q in range(count):
            a_out[p, q] = partial(target, step, lead + q).astype(jnp.bfloat16)
        swaps.append(pltpu.make_async_remote_copy(
            src_ref=a_out.at[p], dst_ref=a_in.at[p], send_sem=a_send.at[p], recv_sem=a_recv.at[p],
            device_id=(b, y * 2 + 1 - core), device_id_type=MESH))
        swaps[-1].start()

    def move(p):
        j, step, lead = pieces[p]
        target = (y + j) % ny * 2 + core
        swaps[p].wait_recv()
        if (j, step) == (0, 0):
            for q in range(count):
                columns = slice((lead + q) * width, (lead + q + 1) * width)
                out_ref[:, columns] = partial(target, step, lead + q) + a_in[p, q].astype(jnp.float32)
            return
        for q in range(count):
            b_out[p, q] = (partial(target, step, lead + q) + a_in[p, q].astype(jnp.float32)).astype(jnp.bfloat16)
        moves.append(pltpu.make_async_remote_copy(
            src_ref=b_out.at[p], dst_ref=b_in.at[p], send_sem=b_send.at[p], recv_sem=b_recv.at[p],
            device_id=(up if step else b, target), device_id_type=MESH))
        moves[-1].start()

    ahead = ny * cuts
    for p in range(ahead):
        swap(p)
    for p in range(len(pieces)):
        move(p)
        if p + ahead < len(pieces):
            swap(p + ahead)
    for p, arrival in enumerate(moves):
        arrival.wait_recv()
        lead = pieces[p][2]
        for q in range(count):
            out_ref[:, (lead + q) * width:(lead + q + 1) * width] += b_in[p, q].astype(jnp.float32)

    for k in range(4):
        @pl.when(sends[k])
        def _(k=k):
            halos[k].wait_send()
    for copy in swaps + moves:
        copy.wait_send()


def shards(atmos_flux, weight_tiles, source_row, target_code, live_count):
    fields, rows, width = atmos_flux.shape
    cap = weight_tiles.shape[2]
    bands, subs = lax.axis_size("band"), lax.axis_size("sub")
    cuts = 2
    pieces = subs * cuts

    table = (-(-(1 + subs) // 8) * 8, 128)
    block = (OB_DEV // cuts, fields, width)
    return pl.pallas_call(
        functools.partial(kernel, (fields, rows, width, cap, bands, subs)),
        out_shape=pltpu.VMEM((fields, OB_DEV * width), jnp.float32),
        in_specs=[
            pl.BlockSpec(memory_space=pltpu.HBM),
            pl.BlockSpec(memory_space=pltpu.HBM),
            pl.BlockSpec(memory_space=pltpu.SMEM),
            pl.BlockSpec(memory_space=pltpu.HBM),
            pl.BlockSpec(memory_space=pltpu.HBM),
        ],
        out_specs=pl.BlockSpec(memory_space=pltpu.VMEM),
        scratch_shapes=[
            pltpu.SMEM((cap,), jnp.int32),
            pltpu.SMEM((cap,), jnp.int32),
            pltpu.VMEM(table, jnp.int32),
            pltpu.SMEM(table, jnp.int32),
            pltpu.VMEM((fields * rows, width), jnp.bfloat16),
            pltpu.VMEM((fields * rows, width), jnp.float32),
            pltpu.VMEM((rows, fields, width), jnp.float32),
            pltpu.VMEM((rows, fields, 3 * width), jnp.bfloat16),
            pltpu.VMEM((cap, 3 * width, width), jnp.bfloat16),
            pltpu.VMEM((cap + 1, fields, width), jnp.float32),
            pltpu.VMEM((4, fields, width), jnp.bfloat16),
            pltpu.VMEM((4, fields, width), jnp.bfloat16),
            pltpu.VMEM((pieces,) + block, jnp.bfloat16),
            pltpu.VMEM((pieces,) + block, jnp.bfloat16),
            pltpu.VMEM((pieces - cuts,) + block, jnp.bfloat16),
            pltpu.VMEM((pieces - cuts,) + block, jnp.bfloat16),
            pltpu.SemaphoreType.DMA((7,)),
            pltpu.SemaphoreType.DMA((4,)),
            pltpu.SemaphoreType.DMA((4,)),
            pltpu.SemaphoreType.DMA((pieces,)),
            pltpu.SemaphoreType.DMA((pieces,)),
            pltpu.SemaphoreType.DMA((pieces - cuts,)),
            pltpu.SemaphoreType.DMA((pieces - cuts,)),
        ],
        compiler_params=pltpu.CompilerParams(
            collective_id=0, has_side_effects=True, vmem_limit_bytes=60 * 1024 * 1024
        ),
    )(source_row[0, 0], target_code[0, 0], live_count, atmos_flux.reshape(fields * rows, width), weight_tiles[0, 0])


def solution(mesh):
    return jax.shard_map(
        shards,
        mesh=mesh,
        in_specs=(
            P(None, "band", "sub"),
            P("band", "sub", None, None, None),
            P("band", "sub", None),
            P("band", "sub", None),
            P("band", "sub"),
        ),
        out_specs=P(None, ("band", "sub")),
        check_vma=False,
    )
```

```python
import functools

import jax
import jax.numpy as jnp
from jax import lax
from jax.experimental import pallas as pl
from jax.experimental.pallas import tpu as pltpu
from jax.sharding import PartitionSpec as P

OB_DEV = 8
MESH = pl.DeviceIdType.MESH


def kernel(
    sizes, row_hbm, code_hbm, live_ref, flux_ref, weight_ref, out_ref,
    row_ref, code_ref, table, found, xin, x32, dx, op, wv, prefix, halo_out, halo_in, a_out, a_in, b_out, b_in,
    in_sem, halo_send, halo_recv, a_send, a_recv, b_send, b_recv,
):
    fields, rows, width, cap, bands, subs = sizes
    ny = subs // 2
    b = lax.axis_index("band")
    s = lax.axis_index("sub")
    y, core = s // 2, s % 2
    up, down = (b + 1) % bands, (b + bands - 1) % bands

    barrier = pltpu.get_barrier_semaphore()
    for other in range(1, subs):
        pl.semaphore_signal(barrier, inc=1, device_id=(b, (s + other) % subs), device_id_type=MESH)
    for other in range(ny):
        pl.semaphore_signal(barrier, inc=1, device_id=(down, other * 2 + core), device_id_type=MESH)

    @pl.when(b < bands - 1)
    def _():
        pl.semaphore_signal(barrier, inc=1, device_id=(up, s), device_id_type=MESH)

    copy_flux = pltpu.make_async_copy(flux_ref, xin, in_sem.at[0])
    copy_flux.start()
    small = []
    for k, (source, place) in enumerate(((code_hbm, code_ref), (row_hbm, row_ref))):
        small.append(pltpu.make_async_copy(source, place, in_sem.at[5 + k]))
        small[-1].start()
    copy_w0 = pltpu.make_async_copy(weight_ref.at[:, :width], wv.at[:, :width], in_sem.at[1])
    copy_w0.start()
    half = cap // 2
    copy_w = []
    for part in range(2):
        where = (pl.ds(part * half, half), pl.ds(width, 2 * width))
        copy_w.append(pltpu.make_async_copy(weight_ref.at[where], wv.at[where], in_sem.at[2 + part]))
        copy_w[-1].start()

    copy_flux.wait()
    x32[...] = xin[...].astype(jnp.float32)
    lane = lax.broadcasted_iota(jnp.int32, (fields, width), 1)

    def row(i):
        return x32[pl.ds(i, fields, stride=rows), :]

    first = jnp.zeros((fields, width), jnp.float32)
    last = jnp.zeros((fields, width), jnp.float32)
    for i in range(rows):
        x = row(i)
        first = jnp.where(lane == i, x[:, :1], first)
        last = jnp.where(lane == i, x[:, width - 1:], last)
    halo_out[0] = row(rows - 1).astype(jnp.bfloat16)
    halo_out[1] = row(0).astype(jnp.bfloat16)
    halo_out[2] = last.astype(jnp.bfloat16)
    halo_out[3] = first.astype(jnp.bfloat16)

    pl.semaphore_wait(barrier, subs - 1 + ny + jnp.where(b > 0, 1, 0))

    partners = ((up, s), (down, s), (b, (s + 1) % subs), (b, (s + subs - 1) % subs))
    sends = (b < bands - 1, b > 0, s < subs - 1, s > 0)
    receives = (b > 0, b < bands - 1, s > 0, s < subs - 1)
    halos = [
        pltpu.make_async_remote_copy(
            src_ref=halo_out.at[k], dst_ref=halo_in.at[k], send_sem=halo_send.at[k], recv_sem=halo_recv.at[k],
            device_id=partners[k], device_id_type=MESH)
        for k in range(4)
    ]
    for k in range(4):
        @pl.when(sends[k])
        def _(k=k):
            halos[k].start()

    for copy in small:
        copy.wait()
    part_row = lax.broadcasted_iota(jnp.int32, table.shape, 0)
    part_lane = lax.broadcasted_iota(jnp.int32, table.shape, 1)
    wanted = jnp.where(part_lane < 2 * OB_DEV, (part_row - 1) * 2 * OB_DEV + part_lane, -1)
    for e in range(cap):
        wanted = jnp.where((part_row == 0) & (part_lane == e), code_ref[e], wanted)
    limit = jnp.where(part_row == 0, part_lane, live_ref[0, 0])
    entry = jnp.full(table.shape, cap, jnp.int32)
    for e in range(cap):
        entry = jnp.where((wanted == code_ref[e]) & (limit > e), e, entry)
    table[...] = entry
    copy_found = pltpu.make_async_copy(table, found, in_sem.at[4])
    copy_found.start()

    for i in range(rows):
        x = row(i)
        op[i, :, :width] = x.astype(jnp.bfloat16)
        east = jnp.where(lane == width - 1, 0.0, pltpu.roll(x, width - 1, 1))
        west = jnp.where(lane == 0, 0.0, pltpu.roll(x, 1, 1))
        dx[i] = east - west
        if 0 < i < rows - 1:
            op[i, :, 2 * width:] = (0.5 * (row(i + 1) - row(i - 1))).astype(jnp.bfloat16)
    prefix[cap] = jnp.zeros((fields, width), jnp.float32)
    copy_w0.wait()

    def flux_part(e, carry):
        picked = op[row_ref[e], :, :width]
        prefix[e] = jnp.dot(picked, wv[e, :width], preferred_element_type=jnp.float32)
        return carry

    lax.fori_loop(0, cap, flux_part, 0, unroll=8)

    for k in range(4):
        @pl.when(receives[k])
        def _(k=k):
            halos[k].wait_recv()

        @pl.when(jnp.logical_not(receives[k]))
        def _(k=k):
            halo_in[k] = jnp.zeros((fields, width), jnp.bfloat16)

    below, above, left, right = (halo_in[k].astype(jnp.float32) for k in range(4))
    for i in range(rows):
        edge = jnp.where(lane == 0, -left[:, i:i + 1], jnp.where(lane == width - 1, right[:, i:i + 1], 0.0))
        op[i, :, width:2 * width] = (0.5 * (dx[i] + edge)).astype(jnp.bfloat16)
    op[0, :, 2 * width:] = (0.5 * (row(1) - below)).astype(jnp.bfloat16)
    op[rows - 1, :, 2 * width:] = (0.5 * (above - row(rows - 2))).astype(jnp.bfloat16)

    def gradient_part(e, carry):
        picked = op[row_ref[e], :, width:]
        product = jnp.dot(picked, wv[e, width:], preferred_element_type=jnp.float32)
        prefix[e] = prefix[e] + product
        return carry

    def chain(e, carry):
        prefix[e] = prefix[e] + prefix[found[0, e]]
        return carry

    for part in range(2):
        copy_w[part].wait()
    lax.fori_loop(0, cap, gradient_part, 0, unroll=16)
    copy_found.wait()
    lax.fori_loop(0, cap, chain, 0, unroll=8)

    def partial(sub, step, q):
        return prefix[found[1 + sub, step * OB_DEV + q]]

    away = [(j, 1) for j in range(1, ny)] + [(0, 1)] + [(j, 0) for j in range(1, ny)] + [(0, 0)]
    count = a_out.shape[1]
    cuts = OB_DEV // count
    pieces = [(j, step, cut * count) for j, step in away for cut in range(cuts)]
    swaps, moves = [], []

    def swap(p):
        j, step, lead = pieces[p]
        target = (y + j) % ny * 2 + 1 - core
        for q in range(count):
            a_out[p, q] = partial(target, step, lead + q).astype(jnp.bfloat16)
        swaps.append(pltpu.make_async_remote_copy(
            src_ref=a_out.at[p], dst_ref=a_in.at[p], send_sem=a_send.at[p], recv_sem=a_recv.at[p],
            device_id=(b, y * 2 + 1 - core), device_id_type=MESH))
        swaps[-1].start()

    def move(p):
        j, step, lead = pieces[p]
        target = (y + j) % ny * 2 + core
        swaps[p].wait_recv()
        if (j, step) == (0, 0):
            for q in range(count):
                columns = slice((lead + q) * width, (lead + q + 1) * width)
                out_ref[:, columns] = partial(target, step, lead + q) + a_in[p, q].astype(jnp.float32)
            return
        for q in range(count):
            b_out[p, q] = (partial(target, step, lead + q) + a_in[p, q].astype(jnp.float32)).astype(jnp.bfloat16)
        moves.append(pltpu.make_async_remote_copy(
            src_ref=b_out.at[p], dst_ref=b_in.at[p], send_sem=b_send.at[p], recv_sem=b_recv.at[p],
            device_id=(up if step else b, target), device_id_type=MESH))
        moves[-1].start()

    ahead = ny * cuts
    for p in range(ahead):
        swap(p)
    for p in range(len(pieces)):
        move(p)
        if p + ahead < len(pieces):
            swap(p + ahead)
    for p, arrival in enumerate(moves):
        arrival.wait_recv()
        lead = pieces[p][2]
        for q in range(count):
            out_ref[:, (lead + q) * width:(lead + q + 1) * width] += b_in[p, q].astype(jnp.float32)

    for k in range(4):
        @pl.when(sends[k])
        def _(k=k):
            halos[k].wait_send()
    for copy in swaps + moves:
        copy.wait_send()


def shards(atmos_flux, weight_tiles, source_row, target_code, live_count):
    fields, rows, width = atmos_flux.shape
    cap = weight_tiles.shape[2]
    bands, subs = lax.axis_size("band"), lax.axis_size("sub")
    cuts = 2
    pieces = subs * cuts

    table = (-(-(1 + subs) // 8) * 8, 128)
    block = (OB_DEV // cuts, fields, width)
    return pl.pallas_call(
        functools.partial(kernel, (fields, rows, width, cap, bands, subs)),
        out_shape=pltpu.VMEM((fields, OB_DEV * width), jnp.float32),
        in_specs=[
            pl.BlockSpec(memory_space=pltpu.HBM),
            pl.BlockSpec(memory_space=pltpu.HBM),
            pl.BlockSpec(memory_space=pltpu.SMEM),
            pl.BlockSpec(memory_space=pltpu.HBM),
            pl.BlockSpec(memory_space=pltpu.HBM),
        ],
        out_specs=pl.BlockSpec(memory_space=pltpu.VMEM),
        scratch_shapes=[
            pltpu.SMEM((cap,), jnp.int32),
            pltpu.SMEM((cap,), jnp.int32),
            pltpu.VMEM(table, jnp.int32),
            pltpu.SMEM(table, jnp.int32),
            pltpu.VMEM((fields * rows, width), jnp.bfloat16),
            pltpu.VMEM((fields * rows, width), jnp.float32),
            pltpu.VMEM((rows, fields, width), jnp.float32),
            pltpu.VMEM((rows, fields, 3 * width), jnp.bfloat16),
            pltpu.VMEM((cap, 3 * width, width), jnp.bfloat16),
            pltpu.VMEM((cap + 1, fields, width), jnp.float32),
            pltpu.VMEM((4, fields, width), jnp.bfloat16),
            pltpu.VMEM((4, fields, width), jnp.bfloat16),
            pltpu.VMEM((pieces,) + block, jnp.bfloat16),
            pltpu.VMEM((pieces,) + block, jnp.bfloat16),
            pltpu.VMEM((pieces - cuts,) + block, jnp.bfloat16),
            pltpu.VMEM((pieces - cuts,) + block, jnp.bfloat16),
            pltpu.SemaphoreType.DMA((7,)),
            pltpu.SemaphoreType.DMA((4,)),
            pltpu.SemaphoreType.DMA((4,)),
            pltpu.SemaphoreType.DMA((pieces,)),
            pltpu.SemaphoreType.DMA((pieces,)),
            pltpu.SemaphoreType.DMA((pieces - cuts,)),
            pltpu.SemaphoreType.DMA((pieces - cuts,)),
        ],
        compiler_params=pltpu.CompilerParams(
            collective_id=0, has_side_effects=True, vmem_limit_bytes=60 * 1024 * 1024
        ),
    )(source_row[0, 0], target_code[0, 0], live_count, atmos_flux.reshape(fields * rows, width), weight_tiles[0, 0])


def solution(mesh):
    return jax.shard_map(
        shards,
        mesh=mesh,
        in_specs=(
            P(None, "band", "sub"),
            P("band", "sub", None, None, None),
            P("band", "sub", None),
            P("band", "sub", None),
            P("band", "sub"),
        ),
        out_specs=P(None, ("band", "sub")),
        check_vma=False,
    )
```

```python
import functools

import jax
import jax.numpy as jnp
from jax import lax
from jax.experimental import pallas as pl
from jax.experimental.pallas import tpu as pltpu
from jax.sharding import PartitionSpec as P

OB_DEV = 8
MESH = pl.DeviceIdType.MESH


def kernel(
    sizes, row_hbm, code_hbm, live_ref, flux_ref, weight_ref, out_ref,
    row_ref, code_ref, table, found, xin, x32, dx, op, wv, prefix, halo_out, halo_in, a_out, a_in, b_out, b_in,
    in_sem, halo_send, halo_recv, a_send, a_recv, b_send, b_recv,
):
    fields, rows, width, cap, bands, subs = sizes
    ny = subs // 2
    b = lax.axis_index("band")
    s = lax.axis_index("sub")
    y, core = s // 2, s % 2
    up, down = (b + 1) % bands, (b + bands - 1) % bands

    barrier = pltpu.get_barrier_semaphore()
    for other in range(1, subs):
        pl.semaphore_signal(barrier, inc=1, device_id=(b, (s + other) % subs), device_id_type=MESH)
    for other in range(ny):
        pl.semaphore_signal(barrier, inc=1, device_id=(down, other * 2 + core), device_id_type=MESH)

    @pl.when(b < bands - 1)
    def _():
        pl.semaphore_signal(barrier, inc=1, device_id=(up, s), device_id_type=MESH)

    copy_flux = pltpu.make_async_copy(flux_ref, xin, in_sem.at[0])
    copy_flux.start()
    small = []
    for k, (source, place) in enumerate(((code_hbm, code_ref), (row_hbm, row_ref))):
        small.append(pltpu.make_async_copy(source, place, in_sem.at[5 + k]))
        small[-1].start()
    copy_w0 = pltpu.make_async_copy(weight_ref.at[:, :width], wv.at[:, :width], in_sem.at[1])
    copy_w0.start()
    half = cap // 2
    copy_w = []
    for part in range(2):
        where = (pl.ds(part * half, half), pl.ds(width, 2 * width))
        copy_w.append(pltpu.make_async_copy(weight_ref.at[where], wv.at[where], in_sem.at[2 + part]))
        copy_w[-1].start()

    copy_flux.wait()
    x32[...] = xin[...].astype(jnp.float32)
    lane = lax.broadcasted_iota(jnp.int32, (fields, width), 1)

    def row(i):
        return x32[pl.ds(i, fields, stride=rows), :]

    first = jnp.zeros((fields, width), jnp.float32)
    last = jnp.zeros((fields, width), jnp.float32)
    for i in range(rows):
        x = row(i)
        first = jnp.where(lane == i, x[:, :1], first)
        last = jnp.where(lane == i, x[:, width - 1:], last)
    halo_out[0] = row(rows - 1).astype(jnp.bfloat16)
    halo_out[1] = row(0).astype(jnp.bfloat16)
    halo_out[2] = last.astype(jnp.bfloat16)
    halo_out[3] = first.astype(jnp.bfloat16)

    pl.semaphore_wait(barrier, subs - 1 + ny + jnp.where(b > 0, 1, 0))

    partners = ((up, s), (down, s), (b, (s + 1) % subs), (b, (s + subs - 1) % subs))
    sends = (b < bands - 1, b > 0, s < subs - 1, s > 0)
    receives = (b > 0, b < bands - 1, s > 0, s < subs - 1)
    halos = [
        pltpu.make_async_remote_copy(
            src_ref=halo_out.at[k], dst_ref=halo_in.at[k], send_sem=halo_send.at[k], recv_sem=halo_recv.at[k],
            device_id=partners[k], device_id_type=MESH)
        for k in range(4)
    ]
    for k in range(4):
        @pl.when(sends[k])
        def _(k=k):
            halos[k].start()

    for copy in small:
        copy.wait()
    part_row = lax.broadcasted_iota(jnp.int32, table.shape, 0)
    part_lane = lax.broadcasted_iota(jnp.int32, table.shape, 1)
    wanted = jnp.where(part_lane < 2 * OB_DEV, (part_row - 1) * 2 * OB_DEV + part_lane, -1)
    for e in range(cap):
        wanted = jnp.where((part_row == 0) & (part_lane == e), code_ref[e], wanted)
    limit = jnp.where(part_row == 0, part_lane, live_ref[0, 0])
    entry = jnp.full(table.shape, cap, jnp.int32)
    for e in range(cap):
        entry = jnp.where((wanted == code_ref[e]) & (limit > e), e, entry)
    table[...] = entry
    copy_found = pltpu.make_async_copy(table, found, in_sem.at[4])
    copy_found.start()

    for i in range(rows):
        x = row(i)
        op[i, :, :width] = x.astype(jnp.bfloat16)
        east = jnp.where(lane == width - 1, 0.0, pltpu.roll(x, width - 1, 1))
        west = jnp.where(lane == 0, 0.0, pltpu.roll(x, 1, 1))
        dx[i] = east - west
        if 0 < i < rows - 1:
            op[i, :, 2 * width:] = (0.5 * (row(i + 1) - row(i - 1))).astype(jnp.bfloat16)
    prefix[cap] = jnp.zeros((fields, width), jnp.float32)
    copy_w0.wait()

    def flux_part(e, carry):
        picked = op[row_ref[e], :, :width]
        prefix[e] = jnp.dot(picked, wv[e, :width], preferred_element_type=jnp.float32)
        return carry

    lax.fori_loop(0, cap, flux_part, 0, unroll=8)

    for k in range(4):
        @pl.when(receives[k])
        def _(k=k):
            halos[k].wait_recv()

        @pl.when(jnp.logical_not(receives[k]))
        def _(k=k):
            halo_in[k] = jnp.zeros((fields, width), jnp.bfloat16)

    below, above, left, right = (halo_in[k].astype(jnp.float32) for k in range(4))
    for i in range(rows):
        edge = jnp.where(lane == 0, -left[:, i:i + 1], jnp.where(lane == width - 1, right[:, i:i + 1], 0.0))
        op[i, :, width:2 * width] = (0.5 * (dx[i] + edge)).astype(jnp.bfloat16)
    op[0, :, 2 * width:] = (0.5 * (row(1) - below)).astype(jnp.bfloat16)
    op[rows - 1, :, 2 * width:] = (0.5 * (above - row(rows - 2))).astype(jnp.bfloat16)

    def gradient_part(e, carry):
        picked = op[row_ref[e], :, width:]
        product = jnp.dot(picked, wv[e, width:], preferred_element_type=jnp.float32)
        prefix[e] = prefix[e] + product
        return carry

    def chain(e, carry):
        prefix[e] = prefix[e] + prefix[found[0, e]]
        return carry

    for part in range(2):
        copy_w[part].wait()
    lax.fori_loop(0, cap, gradient_part, 0, unroll=True)
    copy_found.wait()
    lax.fori_loop(0, cap, chain, 0, unroll=True)

    def partial(sub, step, q):
        return prefix[found[1 + sub, step * OB_DEV + q]]

    away = [(j, 1) for j in range(1, ny)] + [(0, 1)] + [(j, 0) for j in range(1, ny)] + [(0, 0)]
    count = a_out.shape[1]
    cuts = OB_DEV // count
    pieces = [(j, step, cut * count) for j, step in away for cut in range(cuts)]
    swaps, moves = [], []

    def swap(p):
        j, step, lead = pieces[p]
        target = (y + j) % ny * 2 + 1 - core
        for q in range(count):
            a_out[p, q] = partial(target, step, lead + q).astype(jnp.bfloat16)
        swaps.append(pltpu.make_async_remote_copy(
            src_ref=a_out.at[p], dst_ref=a_in.at[p], send_sem=a_send.at[p], recv_sem=a_recv.at[p],
            device_id=(b, y * 2 + 1 - core), device_id_type=MESH))
        swaps[-1].start()

    def move(p):
        j, step, lead = pieces[p]
        target = (y + j) % ny * 2 + core
        swaps[p].wait_recv()
        if (j, step) == (0, 0):
            for q in range(count):
                columns = slice((lead + q) * width, (lead + q + 1) * width)
                out_ref[:, columns] = partial(target, step, lead + q) + a_in[p, q].astype(jnp.float32)
            return
        for q in range(count):
            b_out[p, q] = (partial(target, step, lead + q) + a_in[p, q].astype(jnp.float32)).astype(jnp.bfloat16)
        moves.append(pltpu.make_async_remote_copy(
            src_ref=b_out.at[p], dst_ref=b_in.at[p], send_sem=b_send.at[p], recv_sem=b_recv.at[p],
            device_id=(up if step else b, target), device_id_type=MESH))
        moves[-1].start()

    ahead = ny * cuts
    for p in range(ahead):
        swap(p)
    for p in range(len(pieces)):
        move(p)
        if p + ahead < len(pieces):
            swap(p + ahead)
    for p, arrival in enumerate(moves):
        arrival.wait_recv()
        lead = pieces[p][2]
        for q in range(count):
            out_ref[:, (lead + q) * width:(lead + q + 1) * width] += b_in[p, q].astype(jnp.float32)

    for k in range(4):
        @pl.when(sends[k])
        def _(k=k):
            halos[k].wait_send()
    for copy in swaps + moves:
        copy.wait_send()


def shards(atmos_flux, weight_tiles, source_row, target_code, live_count):
    fields, rows, width = atmos_flux.shape
    cap = weight_tiles.shape[2]
    bands, subs = lax.axis_size("band"), lax.axis_size("sub")
    cuts = 1
    pieces = subs * cuts

    table = (-(-(1 + subs) // 8) * 8, 128)
    block = (OB_DEV // cuts, fields, width)
    return pl.pallas_call(
        functools.partial(kernel, (fields, rows, width, cap, bands, subs)),
        out_shape=pltpu.VMEM((fields, OB_DEV * width), jnp.float32),
        in_specs=[
            pl.BlockSpec(memory_space=pltpu.HBM),
            pl.BlockSpec(memory_space=pltpu.HBM),
            pl.BlockSpec(memory_space=pltpu.SMEM),
            pl.BlockSpec(memory_space=pltpu.HBM),
            pl.BlockSpec(memory_space=pltpu.HBM),
        ],
        out_specs=pl.BlockSpec(memory_space=pltpu.VMEM),
        scratch_shapes=[
            pltpu.SMEM((cap,), jnp.int32),
            pltpu.SMEM((cap,), jnp.int32),
            pltpu.VMEM(table, jnp.int32),
            pltpu.SMEM(table, jnp.int32),
            pltpu.VMEM((fields * rows, width), jnp.bfloat16),
            pltpu.VMEM((fields * rows, width), jnp.float32),
            pltpu.VMEM((rows, fields, width), jnp.float32),
            pltpu.VMEM((rows, fields, 3 * width), jnp.bfloat16),
            pltpu.VMEM((cap, 3 * width, width), jnp.bfloat16),
            pltpu.VMEM((cap + 1, fields, width), jnp.float32),
            pltpu.VMEM((4, fields, width), jnp.bfloat16),
            pltpu.VMEM((4, fields, width), jnp.bfloat16),
            pltpu.VMEM((pieces,) + block, jnp.bfloat16),
            pltpu.VMEM((pieces,) + block, jnp.bfloat16),
            pltpu.VMEM((pieces - cuts,) + block, jnp.bfloat16),
            pltpu.VMEM((pieces - cuts,) + block, jnp.bfloat16),
            pltpu.SemaphoreType.DMA((7,)),
            pltpu.SemaphoreType.DMA((4,)),
            pltpu.SemaphoreType.DMA((4,)),
            pltpu.SemaphoreType.DMA((pieces,)),
            pltpu.SemaphoreType.DMA((pieces,)),
            pltpu.SemaphoreType.DMA((pieces - cuts,)),
            pltpu.SemaphoreType.DMA((pieces - cuts,)),
        ],
        compiler_params=pltpu.CompilerParams(
            collective_id=0, has_side_effects=True, vmem_limit_bytes=60 * 1024 * 1024
        ),
    )(source_row[0, 0], target_code[0, 0], live_count, atmos_flux.reshape(fields * rows, width), weight_tiles[0, 0])


def solution(mesh):
    return jax.shard_map(
        shards,
        mesh=mesh,
        in_specs=(
            P(None, "band", "sub"),
            P("band", "sub", None, None, None),
            P("band", "sub", None),
            P("band", "sub", None),
            P("band", "sub"),
        ),
        out_specs=P(None, ("band", "sub")),
        check_vma=False,
    )
```
